512 devices in a mesh: blk: 32 (over z_hi, y, core), freq: 16 (over x, z_lo).
Axes of the slice: x: 4, y: 4, z: 16 (z_hi: 4, z_lo: 4; z = z_hi * 4 + z_lo), core: 2. Of those that a mesh axis runs over, the one named last changes fastest.
Arguments:
- spectra: bfloat16 [2, 8, 2048, 2048], P(None, None, 'blk', 'freq'), may hold values from -60 to 60
- pairing: int32 [2], replicated, may hold values from 1 to 31, as said below
Outputs:
- lags: float32 [2, 256, 131072], P(None, 'freq', 'blk')
The draws below stay inside these ranges and needn't reach their ends.
Inputs may be any that keep to these rules, and one draw needn't show every extreme that they name: The values of different rounds differ; round r pairs block b with block b XOR pairing[r]; some round holds 31.
All inputs are finite; a program needn't handle non-finite values.
Results may differ from the reference program's by a relative error of at most 0.025.
Values may be sent and summed in bfloat16 or wider, within the bound.
A program may use at most 64 MiB of HBM per device.

```python
import math
import jax
import jax.numpy as jnp
from jax import lax

CB = 64
NB = 2048
L = 256
W = 8
ROUNDS = 2
BLOCKS = 32
CH = 2048
N_FREQ = 16


def draw_spectra(key, part):
    key = jax.random.fold_in(key, 11)
    first_key, scale_key = jax.random.split(key, 2)
    full_shape = (2, W, CH, NB)
    chan_scale = jnp.exp(jax.random.uniform(scale_key, (1, 1, CH, NB), jnp.float32, 0.0, math.log(10.0)))
    values = jnp.clip(jax.random.normal(first_key, full_shape, jnp.float32), -6.0, 6.0)
    return (values * chan_scale).astype(jnp.bfloat16)


def draw_pairing(key, part):
    key = jax.random.fold_in(key, 23)
    order_key, place_key = jax.random.split(key, 2)
    shuffled = jax.random.permutation(order_key, jnp.arange(1, BLOCKS - 1, dtype=jnp.int32))
    position = jax.random.randint(place_key, (), 0, ROUNDS, dtype=jnp.int32)
    round_index = jnp.arange(ROUNDS, dtype=jnp.int32)
    source = round_index - (round_index > position).astype(jnp.int32)
    picked = shuffled[source]
    return jnp.where(round_index == position, BLOCKS - 1, picked).astype(jnp.int32)


def setup_inputs(seed: int = 0) -> dict:
    arg_keys = jax.random.split(jax.random.key(seed), 3)
    spectra = draw_spectra(jax.random.fold_in(arg_keys[2], 71), 0)
    pairing = draw_pairing(jax.random.fold_in(arg_keys[2], 71), 0)
    return {"spectra": spectra, "pairing": pairing}


epsilon = 1e-06

def phase_tables(bin_first, bin_total, lag_total, bin_count):
    bin_index = bin_first + jnp.arange(bin_count, dtype=jnp.int32)
    lag_index = jnp.arange(lag_total, dtype=jnp.int32) - lag_total // 2
    phase_steps = jnp.mod(lag_index[:, None] * bin_index[None, :], 2 * bin_total)
    phase_angle = phase_steps.astype(jnp.float32) * (math.pi / bin_total)
    return jnp.stack([jnp.cos(phase_angle), -jnp.sin(phase_angle)], axis=1)

def reference(spectra, pairing):
    values = spectra.astype(jnp.float32)
    chan_power = lax.optimization_barrier(jnp.sum(values * values, axis=(0, 1))) / W
    white = (values / jnp.sqrt(chan_power + epsilon)).astype(jnp.bfloat16)
    groups = N_FREQ
    bin_count = NB // groups
    lag_table = phase_tables(0, NB, L, NB).astype(jnp.bfloat16)
    lag_table = lax.optimization_barrier(lag_table).astype(jnp.float32)
    lag_table = lag_table.reshape(L, 2, groups, bin_count).transpose(2, 0, 1, 3)
    outputs = []
    for round_index in range(ROUNDS):
        round_mask = pairing[round_index]

        def one_block(block_index):
            partner_index = jnp.bitwise_xor(block_index, round_mask)
            own_part = lax.dynamic_slice_in_dim(white, block_index * CB, CB, 2).astype(jnp.float32)
            mate_part = lax.dynamic_slice_in_dim(white, partner_index * CB, CB, 2).astype(jnp.float32)
            own_stack = jnp.concatenate([own_part[0], own_part[1]], axis=0)
            mate_stack = jnp.stack([jnp.concatenate([mate_part[0], mate_part[1]], axis=0), jnp.concatenate([mate_part[1], -mate_part[0]], axis=0)])
            spectrum = jnp.einsum('wif,cwjf->cfij', own_stack, mate_stack, precision=lax.Precision.HIGHEST) / math.sqrt(W)
            spectrum = lax.optimization_barrier(spectrum.astype(jnp.bfloat16)).astype(jnp.float32)
            spectrum = spectrum.reshape(2, groups, bin_count, CB * CB)
            partials = jnp.einsum('glcf,cgfp->glp', lag_table, spectrum, precision=lax.Precision.HIGHEST) / math.sqrt(NB)
            partials = lax.optimization_barrier(partials.astype(jnp.bfloat16)).astype(jnp.float32)
            return lax.optimization_barrier(jnp.sum(partials, axis=0))
        blocks_out = lax.map(one_block, jnp.arange(BLOCKS, dtype=jnp.int32))
        outputs.append(blocks_out.transpose(1, 0, 2).reshape(L, CH * CB))
    return jnp.stack(outputs)
```

```python
import functools
import math

import jax
import jax.numpy as jnp
from jax import lax
from jax.experimental import pallas as pl
from jax.experimental.pallas import tpu as pltpu
from jax.sharding import PartitionSpec as P

NB = 2048
L = 256
EPS = 1e-06
MESH = pl.DeviceIdType.MESH
ROWS = 272
CK = 4
f32, bf16 = jnp.float32, jnp.bfloat16


def xor(v, mask):
    out = v
    for k in range(5):
        if mask >> k & 1:
            out = out + (1 - 2 * ((v // (1 << k)) % 2)) * (1 << k)
    return out


def phase_table(first, count):
    bins = first + jnp.arange(count, dtype=jnp.int32)
    lags = jnp.arange(ROWS, dtype=jnp.int32) - L // 2
    steps = jnp.mod(lags[:, None] * bins[None, :], 2 * NB)
    angle = steps.astype(f32) * (math.pi / NB)
    return jnp.concatenate([jnp.cos(angle), -jnp.sin(angle)], axis=1).astype(bf16)


def whiten(spectra):
    values = spectra.astype(f32)
    power = jnp.sum(values * values, axis=(0, 1)) / spectra.shape[1]
    return (values / jnp.sqrt(power + EPS)).astype(bf16)


def roles(p, blk):
    low = (p & -p).bit_length() - 1
    return blk % 2, (blk // (1 << low)) % 2


def moves(sends, recvs, locals_, ss, rs):
    barrier = pltpu.get_barrier_semaphore()
    for _, _, source in recvs:
        pl.semaphore_signal(barrier, inc=1, device_id=source, device_id_type=MESH)
    pl.semaphore_wait(barrier, len(sends))
    copies = []
    for n, (src, dst, slot, target) in enumerate(sends):
        copy = pltpu.make_async_remote_copy(
            src_ref=src, dst_ref=dst, send_sem=ss.at[n], recv_sem=rs.at[slot],
            device_id=target, device_id_type=MESH)
        copy.start()
        copies.append(copy)
    for src, dst in locals_:
        dst[...] = src[...]
    for copy in copies:
        copy.wait_send()
    for dst, slot, source in recvs:
        pltpu.make_async_remote_copy(
            src_ref=dst, dst_ref=dst, send_sem=ss.at[0], recv_sem=rs.at[slot],
            device_id=source, device_id_type=MESH).wait_recv()


def exchange_kernel(p, w, m1, m2, ss, rs):
    blk, h = lax.axis_index("blk"), lax.axis_index("freq")
    core, role = roles(p, blk)
    to = lambda mask: (xor(blk, mask), h)
    one = functools.partial(moves, ss=ss, rs=rs)
    if p % 2:
        @pl.when(core == 0)
        def _():
            one([(w, m2, 1, to(p))], [(m2, 1, to(31))], [(w, m1)])

        @pl.when(core == 1)
        def _():
            one([(w, m2, 1, to(31))], [(m2, 1, to(p))], [(w, m1)])
    else:
        @pl.when((core == 0) & (role == 0))
        def _():
            one([(w, m2, 1, to(p ^ 1))], [(m2, 1, to(31))], [(w, m1)])

        @pl.when((core == 0) & (role == 1))
        def _():
            one([(w, m1, 0, to(1))], [(m2, 1, to(31))], [(w, m1)])

        @pl.when((core == 1) & (role == 0))
        def _():
            one([(w, m2, 1, to(31))], [(m2, 1, to(p))], [(w, m1)])

        @pl.when((core == 1) & (role == 1))
        def _():
            one([(w, m2, 1, to(31)), (w, m2, 1, to(p))],
                [(m1, 0, to(1)), (m2, 1, to(p ^ 1))], [])


def result_kernel(p, f, row, za, zb, ra, rb, ss, rs):
    blk, h = lax.axis_index("blk"), lax.axis_index("freq")
    core, role = roles(p, blk)
    flip, turn = 15 - h, (16 - h) % 16
    one = functools.partial(moves, ss=ss, rs=rs)

    def mirror(z, r, slot, mask):
        peer = xor(blk, mask)
        return ([(f, z, slot, (peer, flip)), (row, r, slot + 2, (peer, turn))],
                [(z, slot, (peer, flip)), (r, slot + 2, (peer, turn))])

    a_send, a_recv = mirror(za, ra, 0, 31)
    b_send, b_recv = mirror(zb, rb, 1, p)
    own_a, own_b = [(f, za), (row, ra)], [(f, zb), (row, rb)]
    if p % 2:
        @pl.when(core == 0)
        def _():
            one(a_send, b_recv, own_a)

        @pl.when(core == 1)
        def _():
            one(b_send, a_recv, own_b)
    else:
        c_send, c_recv = mirror(zb, rb, 1, p ^ 1)
        beside = (xor(blk, 1), h)

        @pl.when((core == 0) & (role == 0))
        def _():
            one(a_send, c_recv, own_a)

        @pl.when((core == 0) & (role == 1))
        def _():
            one(a_send, [(zb, 1, beside)], own_a + [(row, rb)])

        @pl.when((core == 1) & (role == 0))
        def _():
            one(b_send, a_recv, own_b)

        @pl.when((core == 1) & (role == 1))
        def _():
            one(c_send + [(f, zb, 1, beside)], a_recv + b_recv, [])


def remote_call(kernel, p, cid, name, shapes, n_send, n_recv, *args):
    spec = pl.BlockSpec(memory_space=pltpu.VMEM)
    return pl.pallas_call(
        functools.partial(kernel, p),
        out_shape=[jax.ShapeDtypeStruct(s, bf16) for s in shapes],
        in_specs=[spec] * len(args),
        out_specs=[spec] * len(shapes),
        scratch_shapes=[pltpu.SemaphoreType.DMA((n_send,)), pltpu.SemaphoreType.DMA((n_recv,))],
        compiler_params=pltpu.CompilerParams(
            collective_id=cid, has_side_effects=True, vmem_limit_bytes=16 << 20),
        name=name,
    )(*args)


def lag_kernel(m1, m2, table, out, row_out, a32, x_buf, part, extra, fwd, rx, summed, rz,
               e_send, e_rx, e_mid, e_rz, ss, fs, rs, zs, zr, es, er, fin):
    blk, h = lax.axis_index("blk"), lax.axis_index("freq")
    x, z = h // 4, h % 4
    xr, xl, xo = (x + 1) % 4, (x + 3) % 4, (x + 2) % 4
    at_x = lambda v: (blk, v * 4 + z)
    zp = [(z + k) % 4 for k in (1, 2, 3)]
    at_z = lambda v: (blk, x * 4 + v)

    barrier = pltpu.get_barrier_semaphore()
    for peer in [at_x(xr), at_x(xl), at_x(xo)] + [at_z(v) for v in zp]:
        pl.semaphore_signal(barrier, inc=1, device_id=peer, device_id_type=MESH)

    a32[...] = m1[...].astype(f32)

    def quad(n, ck, half):
        for ii in range(4):
            i = n * 4 + ii
            rows = [[jnp.broadcast_to(a32[c, w, pl.ds(i, 1), :], (16, 128)).astype(bf16)
                     for w in range(8)] for c in range(2)]
            for jt in range(4):
                js = pl.ds(jt * 16, 16)
                re, im = [], []
                for w in range(8):
                    a0, a1 = rows[0][w], rows[1][w]
                    b0, b1 = m2[0, w, js, :], m2[1, w, js, :]
                    re.append(a0 * b0 + a1 * b1)
                    im.append(a0 * b1 - a1 * b0)
                while len(re) > 1:
                    re = [re[k] + re[k + 1] for k in range(0, len(re), 2)]
                    im = [im[k] + im[k + 1] for k in range(0, len(im), 2)]
                x_buf[pl.ds(ii * 64 + jt * 16, 16), 0:128] = re[0]
                x_buf[pl.ds(ii * 64 + jt * 16, 16), 128:256] = im[0]
        prod = lax.dot_general(table[...], x_buf[...], (((1,), (1,)), ((), ())),
                               preferred_element_type=f32) * (1.0 / 128.0)
        cols = pl.ds(pl.multiple_of((n % 2) * 256, 256), 256)
        part[ck, half, :, :, cols] = prod[0:256].astype(bf16).reshape(4, 64, 256)
        for k in range(2):
            extra[pl.ds(2 * n + k, 1), :] = prod[256:257, k * 128:(k + 1) * 128]

    def copy(src, dst, s, r, peer):
        c = pltpu.make_async_remote_copy(src_ref=src, dst_ref=dst, send_sem=s, recv_sem=r,
                                         device_id=peer, device_id_type=MESH)
        c.start()
        return c

    first, second, third = {}, {}, {}

    def stage0(ck):
        for half in range(2):
            def body(q, carry, half=half):
                quad(ck * 4 + half * 2 + q, ck, half)
                return carry
            lax.fori_loop(0, 2, body, 0)
            if ck == 0 and half == 0:
                pl.semaphore_wait(barrier, 6)
            if half == 0:
                first[ck] = [copy(part.at[ck, 0, xo], fwd.at[ck, 0], fs.at[ck, 0], fs.at[ck, 2], at_x(xr)),
                             copy(part.at[ck, 0, xl], rx.at[ck, 1, 0], ss.at[ck, 0], rs.at[ck, 0], at_x(xl))]
            else:
                first[ck] += [copy(part.at[ck, 1, xo], fwd.at[ck, 1], fs.at[ck, 1], fs.at[ck, 3], at_x(xl)),
                              copy(part.at[ck, 1, xr], rx.at[ck, 0, 1], ss.at[ck, 1], rs.at[ck, 1], at_x(xr))]

    def stage1(ck):
        first[ck][0].wait_recv()
        part[ck, 0, xr] = (part[ck, 0, xr].astype(f32) + fwd[ck, 0].astype(f32)).astype(bf16)
        second[ck] = [copy(part.at[ck, 0, xr], rx.at[ck, 0, 0], ss.at[ck, 2], rs.at[ck, 2], at_x(xr))]
        first[ck][2].wait_recv()
        part[ck, 1, xl] = (part[ck, 1, xl].astype(f32) + fwd[ck, 1].astype(f32)).astype(bf16)
        second[ck] += [copy(part.at[ck, 1, xl], rx.at[ck, 1, 1], ss.at[ck, 3], rs.at[ck, 3], at_x(xl))]

    def stage2(ck):
        first[ck][1].wait_recv()
        first[ck][3].wait_recv()
        second[ck][0].wait_recv()
        second[ck][1].wait_recv()
        for half in range(2):
            total = (part[ck, half, x].astype(f32) + rx[ck, 0, half].astype(f32)
                     + rx[ck, 1, half].astype(f32))
            summed[ck, :, :, half * 512:(half + 1) * 512] = total.astype(bf16).reshape(4, 16, 512)
        third[ck] = [copy(summed.at[ck, zp[k]], rz.at[ck, 2 - k], zs.at[ck, k], zr.at[ck, 2 - k], at_z(zp[k]))
                     for k in range(3)]

    def stage3(ck):
        for c in third[ck]:
            c.wait_recv()
        total = (summed[ck, z].astype(f32) + rz[ck, 0].astype(f32) + rz[ck, 1].astype(f32)
                 + rz[ck, 2].astype(f32))
        out[:, ck * 1024:(ck + 1) * 1024] = total.astype(bf16)
        for n in range(8):
            fin[ck * 8 + n:ck * 8 + n + 1, :] = total[0:1, n * 128:(n + 1) * 128]

    for step in range(CK + 3):
        if step < CK:
            stage0(step)
            if step == CK - 1:
                e_send[...] = extra[...].astype(bf16)
                edge = [copy(e_send, e_rx.at[k], es.at[k], er.at[k], at_x(v))
                        for k, v in enumerate((xr, xl, xo))]
        if 0 <= step - 1 < CK:
            stage1(step - 1)
        if 0 <= step - 2 < CK:
            stage2(step - 2)
        if step == CK:
            for c in edge:
                c.wait_recv()
            e_mid[...] = (e_send[...].astype(f32) + e_rx[0].astype(f32) + e_rx[1].astype(f32)
                          + e_rx[2].astype(f32)).astype(bf16)
            edge_z = [copy(e_mid, e_rz.at[2 - k], es.at[3 + k], er.at[3 + 2 - k], at_z(zp[k]))
                      for k in range(3)]
        if 0 <= step - 3 < CK:
            stage3(step - 3)
    for c in edge_z:
        c.wait_recv()
    last = (e_mid[...].astype(f32) + e_rz[0].astype(f32) + e_rz[1].astype(f32)
            + e_rz[2].astype(f32))
    row_out[...] = jnp.where(h == 0, last, fin[...]).astype(bf16)
    for ck in range(CK):
        for c in first[ck] + second[ck] + third[ck]:
            c.wait_send()
    for c in edge + edge_z:
        c.wait_send()


def lag_call(m1, m2, table, cid):
    spec = pl.BlockSpec(memory_space=pltpu.VMEM)
    dma = pltpu.SemaphoreType.DMA
    return pl.pallas_call(
        lag_kernel,
        out_shape=[jax.ShapeDtypeStruct((16, 4096), bf16), jax.ShapeDtypeStruct((32, 128), bf16)],
        in_specs=[spec] * 3,
        out_specs=[spec] * 2,
        scratch_shapes=[
            pltpu.VMEM((2, 8, 64, 128), f32),
            pltpu.VMEM((256, 256), bf16),
            pltpu.VMEM((CK, 2, 4, 64, 512), bf16),
            pltpu.VMEM((32, 128), f32),
            pltpu.VMEM((CK, 2, 64, 512), bf16),
            pltpu.VMEM((CK, 2, 2, 64, 512), bf16),
            pltpu.VMEM((CK, 4, 16, 1024), bf16),
            pltpu.VMEM((CK, 3, 16, 1024), bf16),
            pltpu.VMEM((32, 128), bf16),
            pltpu.VMEM((3, 32, 128), bf16),
            pltpu.VMEM((32, 128), bf16),
            pltpu.VMEM((3, 32, 128), bf16),
            dma((CK, 4)), dma((CK, 4)), dma((CK, 4)), dma((CK, 3)), dma((CK, 3)),
            dma((6,)), dma((6,)),
            pltpu.VMEM((32, 128), f32),
        ],
        compiler_params=pltpu.CompilerParams(
            collective_id=cid, has_side_effects=True, vmem_limit_bytes=32 << 20),
        name="lags",
    )(m1, m2, table)


def transposed(z, row):
    wide = jnp.concatenate([row.reshape(1, 4096), z[:0:-1]], axis=0)
    return wide.reshape(16, 64, 64).transpose(0, 2, 1).reshape(16, 4096)


def on_device(spectra, pairing):
    bins = spectra.shape[3]
    blk, h = lax.axis_index("blk"), lax.axis_index("freq")
    white = whiten(spectra)
    table = phase_table(h * bins, bins)
    other = pairing[0] + pairing[1] - 31
    block = white.shape

    def exchange(p):
        return lambda w: tuple(remote_call(exchange_kernel, p, p - 1, "exchange",
                                           [block, block], 2, 2, w))

    def results(p):
        return lambda f, r: tuple(remote_call(
            result_kernel, p, 30 + p, "results",
            [(16, 4096), (16, 4096), (32, 128), (32, 128)], 3, 4, f, r))

    m1, m2 = lax.switch(other - 1, [exchange(p) for p in range(1, 31)], white)
    final, row = lag_call(m1, m2, table, 30)
    za, zb, ra, rb = lax.switch(other - 1, [results(p) for p in range(1, 31)], final, row)

    core = blk % 2
    low = other & -other
    role = ((blk & low) != 0).astype(jnp.int32)
    plain_a = core == 0
    plain_b = jnp.where(other % 2 == 1, core == 1, core != role)
    out_a = jnp.where(plain_a, za, transposed(za, ra))
    out_b = jnp.where(plain_b, zb, transposed(zb, rb))
    first = pairing[0] == 31
    return jnp.stack([jnp.where(first, out_a, out_b), jnp.where(first, out_b, out_a)]).astype(f32)


def solution(mesh):
    in_specs = (P(None, None, "blk", "freq"), P())
    out_specs = P(None, "freq", "blk")
    return jax.shard_map(
        on_device, mesh=mesh, in_specs=in_specs, out_specs=out_specs, check_vma=False
    )
```

```python
import functools
import math

import jax
import jax.numpy as jnp
from jax import lax
from jax.experimental import pallas as pl
from jax.experimental.pallas import tpu as pltpu
from jax.sharding import PartitionSpec as P

NB = 2048
L = 256
EPS = 1e-06
MESH = pl.DeviceIdType.MESH
ROWS = 272
CK = 4
CC = 4096 // CK
CH = CC // 64
f32, bf16 = jnp.float32, jnp.bfloat16


def xor(v, mask):
    out = v
    for k in range(5):
        if mask >> k & 1:
            out = out + (1 - 2 * ((v // (1 << k)) % 2)) * (1 << k)
    return out


def kernel(p, w_buf, table, z, r, m1, m2, m32, x_buf, part, extra, fwd, rx, summed, rz,
           f_buf, row, fin, e_send, e_rx, e_mid, e_rz,
           m1_s, m2_s, m1_r, m2_r, ss, fs, rs, zs, zr, es, er, os, orr, ws, wr):
    blk, h = lax.axis_index("blk"), lax.axis_index("freq")
    core = blk % 2
    odd = p % 2 == 1
    low = (p & -p).bit_length() - 1
    role = (blk // (1 << low)) % 2
    late = (core == 1) & (role == 1)
    gives = (core == 0) & (role == 1)
    peer_b = xor(blk, p) if odd else (1 - role) * xor(blk, p) + role * xor(blk, p ^ 1)
    peer = (1 - core) * xor(blk, 31) + core * peer_b
    beside = xor(blk, 1)
    flip, turn = 15 - h, (16 - h) % 16
    x, zl = h // 4, h % 4
    xr, xl, xo = (x + 1) % 4, (x + 3) % 4, (x + 2) % 4
    at_x = lambda v: (blk, v * 4 + zl)
    zp = [(zl + k) % 4 for k in (1, 2, 3)]
    at_z = lambda v: (blk, x * 4 + v)

    to_a = xor(blk, 31)
    to_b = xor(blk, p) if odd else xor(blk, p ^ 1)
    m2_to = core * to_a + (1 - core) * to_b

    barrier = pltpu.get_barrier_semaphore()

    def greet(peer):
        pl.semaphore_signal(barrier, inc=1, device_id=peer, device_id_type=MESH)

    for q in [at_x(xr), at_x(xl), at_x(xo)] + [at_z(v) for v in zp] + [(peer, h)]:
        greet(q)
    if odd:
        greet((m2_to, flip))
        greet((m2_to, turn))
    else:
        @pl.when(jnp.logical_not(gives))
        def _():
            greet((m2_to, flip))
            greet((m2_to, turn))

        @pl.when(gives)
        def _():
            greet((beside, h))

        @pl.when(late)
        def _():
            greet((beside, h))
            greet((xor(blk, p), flip))
            greet((xor(blk, p), turn))

    if odd:
        pl.semaphore_wait(barrier, 9)
        m1[...] = w_buf[...]
    else:
        @pl.when(late)
        def _():
            pl.semaphore_wait(barrier, 11)

        @pl.when(jnp.logical_not(late))
        def _():
            pl.semaphore_wait(barrier, 9)
            m1[...] = w_buf[...]

    def copy(src, dst, s, r, peer, start=True):
        c = pltpu.make_async_remote_copy(src_ref=src, dst_ref=dst, send_sem=s, recv_sem=r,
                                         device_id=peer, device_id_type=MESH)
        if start:
            c.start()
        return c

    def chunk(ck, n, target, start=True):
        piece = pl.ds(ck * CH, CH)
        return copy(w_buf.at[:, :, piece], m2.at[:, :, piece], m2_s.at[n, ck], m2_r.at[ck],
                    (target, h), start)

    def whole(start=True):
        return copy(w_buf, m1, m1_s, m1_r, (beside, h), start)

    if odd:
        for ck in range(CK):
            chunk(ck, 0, m2_to)
    else:
        @pl.when(gives)
        def _():
            whole()

        @pl.when(jnp.logical_not(gives))
        def _():
            for ck in range(CK):
                chunk(ck, 0, m2_to)

        @pl.when(late)
        def _():
            for ck in range(CK):
                chunk(ck, 1, xor(blk, p))

    if not odd:
        @pl.when(late)
        def _():
            whole(False).wait_recv()

    def quad(n, ck, half):
        def row(jj, carry):
            j = pl.ds((n % (CH // 4)) * 4 + jj, 1)
            b = jnp.broadcast_to(m32[:, :, j, :], (2, 8, 64, 128)).astype(bf16)
            a = m1[...]
            re = a[0] * b[0] + a[1] * b[1]
            im = a[0] * b[1] - a[1] * b[0]
            to = pl.ds(pl.multiple_of(jj * 64, 64), 64)
            for k, part_ in ((0, re), (128, im)):
                part_ = part_[:4] + part_[4:]
                part_ = part_[:2] + part_[2:]
                x_buf[to, k:k + 128] = part_[0] + part_[1]
            return carry

        lax.fori_loop(0, 4, row, 0, unroll=False)
        prod = lax.dot_general(table[...], x_buf[...], (((1,), (1,)), ((), ())),
                               preferred_element_type=f32) * (1.0 / 128.0)
        cols = pl.ds(pl.multiple_of((n % (CC // 512)) * 256, 256), 256)
        part[ck, half, :, :, cols] = prod[0:256].astype(bf16).reshape(4, 64, 256)
        for k in range(2):
            extra[pl.ds(2 * n + k, 1), :] = prod[256:257, k * 128:(k + 1) * 128]

    first, second, third, fourth = {}, {}, {}, {}
    HALF = CC // 2
    QUADS = CC // 512

    def stage0(ck):
        chunk(ck, 0, peer, False).wait_recv()
        m32[...] = m2[:, :, ck * CH:(ck + 1) * CH, :].astype(f32)
        for half in range(2):
            def body(q, carry, half=half):
                quad(ck * 2 * QUADS + half * QUADS + q, ck, half)
                return carry
            lax.fori_loop(0, QUADS, body, 0)
            if half == 0:
                first[ck] = [copy(part.at[ck, 0, xo], fwd.at[ck, 0], fs.at[ck, 0], fs.at[ck, 2], at_x(xr)),
                             copy(part.at[ck, 0, xl], rx.at[ck, 1, 0], ss.at[ck, 0], rs.at[ck, 0], at_x(xl))]
            else:
                first[ck] += [copy(part.at[ck, 1, xo], fwd.at[ck, 1], fs.at[ck, 1], fs.at[ck, 3], at_x(xl)),
                              copy(part.at[ck, 1, xr], rx.at[ck, 0, 1], ss.at[ck, 1], rs.at[ck, 1], at_x(xr))]

    def stage1(ck):
        first[ck][0].wait_recv()
        part[ck, 0, xr] = (part[ck, 0, xr].astype(f32) + fwd[ck, 0].astype(f32)).astype(bf16)
        second[ck] = [copy(part.at[ck, 0, xr], rx.at[ck, 0, 0], ss.at[ck, 2], rs.at[ck, 2], at_x(xr))]
        first[ck][2].wait_recv()
        part[ck, 1, xl] = (part[ck, 1, xl].astype(f32) + fwd[ck, 1].astype(f32)).astype(bf16)
        second[ck] += [copy(part.at[ck, 1, xl], rx.at[ck, 1, 1], ss.at[ck, 3], rs.at[ck, 3], at_x(xl))]

    def stage2(ck):
        first[ck][1].wait_recv()
        first[ck][3].wait_recv()
        second[ck][0].wait_recv()
        second[ck][1].wait_recv()
        for half in range(2):
            total = (part[ck, half, x].astype(f32) + rx[ck, 0, half].astype(f32)
                     + rx[ck, 1, half].astype(f32))
            summed[ck, :, :, half * HALF:(half + 1) * HALF] = total.astype(bf16).reshape(4, 16, HALF)
        third[ck] = [copy(summed.at[ck, zp[k]], rz.at[ck, 2 - k], zs.at[ck, k], zr.at[ck, 2 - k], at_z(zp[k]))
                     for k in range(3)]

    def result(ck, n, target, start=True):
        cols = pl.ds(ck * CC, CC)
        return copy(f_buf.at[:, cols], z.at[core, :, cols], os.at[n, ck], orr.at[core, ck], target, start)

    def got(ck, slot):
        cols = pl.ds(ck * CC, CC)
        copy(f_buf.at[:, cols], z.at[slot, :, cols], os.at[0, ck], orr.at[slot, ck],
             (peer, flip), False).wait_recv()

    def stage3(ck):
        for c in third[ck]:
            c.wait_recv()
        total = (summed[ck, zl].astype(f32) + rz[ck, 0].astype(f32) + rz[ck, 1].astype(f32)
                 + rz[ck, 2].astype(f32))
        value = total.astype(bf16)
        f_buf[:, ck * CC:(ck + 1) * CC] = value
        fourth[ck] = [result(ck, 0, (peer, flip))]
        if odd:
            z[core, :, ck * CC:(ck + 1) * CC] = value
        else:
            @pl.when(late)
            def _():
                result(ck, 1, (beside, h))

            @pl.when(jnp.logical_not(late))
            def _():
                z[core, :, ck * CC:(ck + 1) * CC] = value
        for n in range(CC // 128):
            fin[ck * (CC // 128) + n:ck * (CC // 128) + n + 1, :] = total[0:1, n * 128:(n + 1) * 128]

    for step in range(CK + 3):
        if step < CK:
            stage0(step)
            if step == CK - 1:
                e_send[...] = extra[...].astype(bf16)
                edge = [copy(e_send, e_rx.at[k], es.at[k], er.at[k], at_x(v))
                        for k, v in enumerate((xr, xl, xo))]
        if 0 <= step - 1 < CK:
            stage1(step - 1)
        if 0 <= step - 2 < CK:
            stage2(step - 2)
        if step == CK:
            for c in edge:
                c.wait_recv()
            e_mid[...] = (e_send[...].astype(f32) + e_rx[0].astype(f32) + e_rx[1].astype(f32)
                          + e_rx[2].astype(f32)).astype(bf16)
            edge_z = [copy(e_mid, e_rz.at[2 - k], es.at[3 + k], er.at[3 + 2 - k], at_z(zp[k]))
                      for k in range(3)]
        if step == CK + 2:
            for c in edge_z:
                c.wait_recv()
        if 0 <= step - 3 < CK:
            stage3(step - 3)
    last = (e_mid[...].astype(f32) + e_rz[0].astype(f32) + e_rz[1].astype(f32)
            + e_rz[2].astype(f32))
    row[...] = jnp.where(h == 0, last, fin[...]).astype(bf16)
    tail = copy(row, r.at[core], ws, wr.at[core], (peer, turn))
    other = 1 - core

    def got_row(slot):
        copy(row, r.at[slot], ws, wr.at[slot], (peer, turn), False).wait_recv()

    if odd:
        r[core] = row[...]
        got_row(other)
    else:
        @pl.when(jnp.logical_not(late))
        def _():
            r[core] = row[...]

        @pl.when(gives)
        def _():
            r[1] = row[...]

        @pl.when(jnp.logical_not(gives))
        def _():
            got_row(other)

        @pl.when(late)
        def _():
            got_row(1)
    for ck in range(CK):
        got(ck, other)
    if not odd:
        @pl.when(late)
        def _():
            for ck in range(CK):
                got(ck, 1)
                result(ck, 1, (beside, h), False).wait_send()
                chunk(ck, 1, xor(blk, p), False).wait_send()

        @pl.when(gives)
        def _():
            whole(False).wait_send()

        @pl.when(jnp.logical_not(gives))
        def _():
            for ck in range(CK):
                chunk(ck, 0, m2_to, False).wait_send()
    else:
        for ck in range(CK):
            chunk(ck, 0, m2_to, False).wait_send()
    for ck in range(CK):
        for c in first[ck] + second[ck] + third[ck] + fourth[ck]:
            c.wait_send()
    for c in edge + edge_z + [tail]:
        c.wait_send()


def call(p, white, table):
    spec = pl.BlockSpec(memory_space=pltpu.VMEM)
    dma = pltpu.SemaphoreType.DMA
    return tuple(pl.pallas_call(
        functools.partial(kernel, p),
        out_shape=[jax.ShapeDtypeStruct((2, 16, 4096), bf16), jax.ShapeDtypeStruct((2, 32, 128), bf16)],
        in_specs=[spec] * 2,
        out_specs=[spec] * 2,
        scratch_shapes=[
                pltpu.VMEM((2, 8, 64, 128), bf16),
            pltpu.VMEM((2, 8, 64, 128), bf16),
            pltpu.VMEM((2, 8, CH, 128), f32),
            pltpu.VMEM((256, 256), bf16),
            pltpu.VMEM((CK, 2, 4, 64, CC // 2), bf16),
            pltpu.VMEM((32, 128), f32),
            pltpu.VMEM((CK, 2, 64, CC // 2), bf16),
            pltpu.VMEM((CK, 2, 2, 64, CC // 2), bf16),
            pltpu.VMEM((CK, 4, 16, CC), bf16),
            pltpu.VMEM((CK, 3, 16, CC), bf16),
            pltpu.VMEM((16, 4096), bf16),
            pltpu.VMEM((32, 128), bf16),
            pltpu.VMEM((32, 128), f32),
            pltpu.VMEM((32, 128), bf16),
            pltpu.VMEM((3, 32, 128), bf16),
            pltpu.VMEM((32, 128), bf16),
            pltpu.VMEM((3, 32, 128), bf16),
            dma, dma((2, CK)), dma, dma((CK,)),
            dma((CK, 4)), dma((CK, 4)), dma((CK, 4)), dma((CK, 3)), dma((CK, 3)),
            dma((6,)), dma((6,)), dma((2, CK)), dma((2, CK)), dma, dma((2,)),
        ],
        compiler_params=pltpu.CompilerParams(
            collective_id=p - 1, has_side_effects=True, vmem_limit_bytes=32 << 20),
        name="fused",
    )(white, table))


def phase_table(first, count):
    bins = first + jnp.arange(count, dtype=jnp.int32)
    lags = jnp.arange(ROWS, dtype=jnp.int32) - L // 2
    steps = jnp.mod(lags[:, None] * bins[None, :], 2 * NB)
    angle = steps.astype(f32) * (math.pi / NB)
    return jnp.concatenate([jnp.cos(angle), -jnp.sin(angle)], axis=1).astype(bf16)


def whiten(spectra):
    values = spectra.astype(f32)
    power = jnp.sum(values * values, axis=(0, 1)) / spectra.shape[1]
    return (values / jnp.sqrt(power + EPS)).astype(bf16)


def on_device(spectra, pairing):
    blk = lax.axis_index("blk")
    white = whiten(spectra)
    table = phase_table(lax.axis_index("freq") * 128, 128)
    other = pairing[0] + pairing[1] - 31
    z, r = lax.switch(other - 1, [functools.partial(call, p) for p in range(1, 31)], white, table)

    def plain(k):
        return z[k].reshape(16, 64, 64).transpose(0, 2, 1).reshape(16, 4096)

    def mirrored(k):
        return jnp.concatenate([r[k].reshape(1, 4096), z[k, :0:-1]], axis=0)

    core = blk % 2
    role = ((blk & other & -other) != 0).astype(jnp.int32)
    plain_b = jnp.where(other % 2 == 1, core == 1, core != role)
    out_a = jnp.where(core == 0, plain(0), mirrored(0))
    out_b = jnp.where(plain_b, plain(1), mirrored(1))
    lead = pairing[0] == 31
    return jnp.stack([jnp.where(lead, out_a, out_b), jnp.where(lead, out_b, out_a)]).astype(f32)


def solution(mesh):
    in_specs = (P(None, None, "blk", "freq"), P())
    out_specs = P(None, "freq", "blk")
    return jax.shard_map(
        on_device, mesh=mesh, in_specs=in_specs, out_specs=out_specs, check_vma=False
    )
```

```python
import functools
import math

import jax
import jax.numpy as jnp
from jax import lax
from jax.experimental import pallas as pl
from jax.experimental.pallas import tpu as pltpu
from jax.sharding import PartitionSpec as P

NB = 2048
L = 256
EPS = 1e-06
MESH = pl.DeviceIdType.MESH
ROWS = 272
CK = 4
CC = 4096 // CK
CH = CC // 64
f32, bf16 = jnp.float32, jnp.bfloat16


def xor(v, mask):
    out = v
    for k in range(5):
        if mask >> k & 1:
            out = out + (1 - 2 * ((v // (1 << k)) % 2)) * (1 << k)
    return out


def kernel(p, w_buf, table, z, r, m1, m2, m32, x_buf, part, extra, fwd, rx, summed, rz,
           f_buf, row, fin, e_send, e_rx, e_mid, e_rz,
           m1_s, m2_s, m1_r, m2_r, ss, fs, rs, zs, zr, es, er, os, orr, ws, wr):
    blk, h = lax.axis_index("blk"), lax.axis_index("freq")
    core = blk % 2
    odd = p % 2 == 1
    low = (p & -p).bit_length() - 1
    role = (blk // (1 << low)) % 2
    late = (core == 1) & (role == 1)
    gives = (core == 0) & (role == 1)
    peer_b = xor(blk, p) if odd else (1 - role) * xor(blk, p) + role * xor(blk, p ^ 1)
    peer = (1 - core) * xor(blk, 31) + core * peer_b
    beside = xor(blk, 1)
    flip, turn = 15 - h, (16 - h) % 16
    x, zl = h // 4, h % 4
    xr, xl, xo = (x + 1) % 4, (x + 3) % 4, (x + 2) % 4
    at_x = lambda v: (blk, v * 4 + zl)
    zp = [(zl + k) % 4 for k in (1, 2, 3)]
    at_z = lambda v: (blk, x * 4 + v)

    to_a = xor(blk, 31)
    to_b = xor(blk, p) if odd else xor(blk, p ^ 1)
    m2_to = core * to_a + (1 - core) * to_b

    barrier = pltpu.get_barrier_semaphore()

    def greet(peer):
        pl.semaphore_signal(barrier, inc=1, device_id=peer, device_id_type=MESH)

    for q in [at_x(xr), at_x(xl), at_x(xo)] + [at_z(v) for v in zp] + [(peer, h)]:
        greet(q)
    if odd:
        greet((m2_to, flip))
        greet((m2_to, turn))
    else:
        @pl.when(jnp.logical_not(gives))
        def _():
            greet((m2_to, flip))
            greet((m2_to, turn))

        @pl.when(gives)
        def _():
            greet((beside, h))

        @pl.when(late)
        def _():
            greet((beside, h))
            greet((xor(blk, p), flip))
            greet((xor(blk, p), turn))

    if odd:
        pl.semaphore_wait(barrier, 9)
        m1[...] = w_buf[...]
    else:
        @pl.when(late)
        def _():
            pl.semaphore_wait(barrier, 11)

        @pl.when(jnp.logical_not(late))
        def _():
            pl.semaphore_wait(barrier, 9)
            m1[...] = w_buf[...]

    def copy(src, dst, s, r, peer, start=True):
        c = pltpu.make_async_remote_copy(src_ref=src, dst_ref=dst, send_sem=s, recv_sem=r,
                                         device_id=peer, device_id_type=MESH)
        if start:
            c.start()
        return c

    def loop(count, do):
        def one(k, carry):
            do(k)
            return carry
        lax.fori_loop(0, count, one, 0)

    def chunk(ck, n, target, start=True, at=None):
        piece = pl.ds(ck * CH if isinstance(ck, int) else pl.multiple_of(ck * CH, CH), CH)
        to = ck if at is None else at
        return copy(w_buf.at[:, :, piece], m2.at[to], m2_s.at[n, to], m2_r.at[to],
                    (target, h), start)

    def whole(start=True):
        return copy(w_buf, m1, m1_s, m1_r, (beside, h), start)

    def give(n, target):
        loop(CK, lambda ck: chunk(ck, n, target) and None)

    if odd:
        give(0, m2_to)
    else:
        @pl.when(gives)
        def _():
            whole()

        @pl.when(jnp.logical_not(gives))
        def _():
            give(0, m2_to)

        @pl.when(late)
        def _():
            give(1, xor(blk, p))

    if not odd:
        @pl.when(late)
        def _():
            whole(False).wait_recv()

    HALF = CC // 2
    QUADS = CC // 512

    def quad(q, ck):
        def row(jj, carry):
            b = jnp.broadcast_to(m32[:, :, pl.ds(q * 4 + jj, 1), :], (2, 8, 64, 128)).astype(bf16)
            a = m1[...]
            re = a[0] * b[0] + a[1] * b[1]
            im = a[0] * b[1] - a[1] * b[0]
            to = pl.ds(pl.multiple_of(jj * 64, 64), 64)
            for k, part_ in ((0, re), (128, im)):
                part_ = part_[:4] + part_[4:]
                part_ = part_[:2] + part_[2:]
                x_buf[to, k:k + 128] = part_[0] + part_[1]
            return carry

        lax.fori_loop(0, 4, row, 0, unroll=False)
        cols = pl.ds(pl.multiple_of((q % QUADS) * 256, 256), 256)

        prod = lax.dot_general(table[...], x_buf[...], (((1,), (1,)), ((), ())),
                               preferred_element_type=f32) * (1.0 / 128.0)
        part[ck, q // QUADS, :, :, cols] = prod[0:256].astype(bf16).reshape(4, 64, 256)
        for k in range(2):
            extra[pl.ds(2 * (ck * 2 * QUADS + q) + k, 1), :] = prod[256:257, k * 128:(k + 1) * 128]

    def ahead(ck, start, half):
        to = (x + 1 + 2 * half) % 4
        return copy(part.at[ck, half, xo], fwd.at[ck, half], fs.at[ck, half], fs.at[ck, 2 + half],
                    at_x(to), start)

    def direct(ck, start, half):
        to = (x + 3 + 2 * half) % 4
        return copy(part.at[ck, half, to], rx.at[ck, 1 - half, half], ss.at[ck, half],
                    rs.at[ck, half], at_x(to), start)

    def onward(ck, start, half):
        to = (x + 1 + 2 * half) % 4
        return copy(part.at[ck, half, to], rx.at[ck, half, half], ss.at[ck, 2 + half],
                    rs.at[ck, 2 + half], at_x(to), start)

    def along(ck, start, k):
        to = (zl + 1 + k) % 4
        return copy(summed.at[ck, to], rz.at[ck, 2 - k], zs.at[ck, k], zr.at[ck, 2 - k], at_z(to), start)

    def columns(ck):
        return pl.ds(ck * CC if isinstance(ck, int) else pl.multiple_of(ck * CC, CC), CC)

    def result(ck, n, target, start=True):
        cols = columns(ck)
        return copy(f_buf.at[:, cols], z.at[core, :, cols], os.at[n, ck], orr.at[core, ck], target, start)

    def got(ck, slot):
        cols = columns(ck)
        copy(f_buf.at[:, cols], z.at[slot, :, cols], os.at[0, ck], orr.at[slot, ck],
             (peer, flip), False).wait_recv()

    def stage0(ck):
        chunk(0, 0, peer, False, at=ck).wait_recv()
        m32[...] = m2[ck].astype(f32)

        def body(q, carry):
            quad(q, ck)

            @pl.when(q % QUADS == QUADS - 1)
            def _():
                ahead(ck, True, q // QUADS)
                direct(ck, True, q // QUADS)

            return carry

        lax.fori_loop(0, 2 * QUADS, body, 0)

    def stage1(ck):
        def half_(half):
            to = (x + 1 + 2 * half) % 4
            ahead(ck, False, half).wait_recv()
            part[ck, half, to] = (part[ck, half, to].astype(f32) + fwd[ck, half].astype(f32)).astype(bf16)
            onward(ck, True, half)

        loop(2, half_)

    def stage2(ck):
        def half_(half):
            direct(ck, False, half).wait_recv()
            onward(ck, False, half).wait_recv()

        loop(2, half_)

        def add(half):
            total = (part[ck, half, x].astype(f32) + rx[ck, 0, half].astype(f32)
                     + rx[ck, 1, half].astype(f32))
            to = pl.ds(pl.multiple_of(half * HALF, HALF), HALF)
            summed[ck, :, :, to] = total.astype(bf16).reshape(4, 16, HALF)

        loop(2, add)
        loop(3, lambda k: along(ck, True, k) and None)

    def stage3(ck):
        loop(3, lambda k: along(ck, False, k).wait_recv())
        total = (summed[ck, zl].astype(f32) + rz[ck, 0].astype(f32) + rz[ck, 1].astype(f32)
                 + rz[ck, 2].astype(f32))
        value = total.astype(bf16)
        f_buf[:, columns(ck)] = value
        result(ck, 0, (peer, flip))
        if odd:
            z[core, :, columns(ck)] = value
        else:
            @pl.when(late)
            def _():
                result(ck, 1, (beside, h))

            @pl.when(jnp.logical_not(late))
            def _():
                z[core, :, columns(ck)] = value
        for n in range(CC // 128):
            fin[pl.ds(ck * (CC // 128) + n, 1), :] = total[0:1, n * 128:(n + 1) * 128]

    def edge(start, k):
        return copy(e_send, e_rx.at[k], es.at[k], er.at[k], at_x((x + 1 + k) % 4), start)

    def edge_z(start, k):
        return copy(e_mid, e_rz.at[2 - k], es.at[3 + k], er.at[5 - k], at_z((zl + 1 + k) % 4), start)

    def step_body(step, carry):
        @pl.when(step < CK)
        def _():
            stage0(step)

        @pl.when(step == CK - 1)
        def _():
            e_send[...] = extra[...].astype(bf16)
            loop(3, lambda k: edge(True, k) and None)

        @pl.when((step >= 1) & (step < CK + 1))
        def _():
            stage1(step - 1)

        @pl.when((step >= 2) & (step < CK + 2))
        def _():
            stage2(step - 2)

        @pl.when(step == CK)
        def _():
            loop(3, lambda k: edge(False, k).wait_recv())
            e_mid[...] = (e_send[...].astype(f32) + e_rx[0].astype(f32) + e_rx[1].astype(f32)
                          + e_rx[2].astype(f32)).astype(bf16)
            loop(3, lambda k: edge_z(True, k) and None)

        @pl.when(step >= 3)
        def _():
            stage3(step - 3)

        return carry

    lax.fori_loop(0, CK + 3, step_body, 0)
    loop(3, lambda k: edge_z(False, k).wait_recv())
    last = (e_mid[...].astype(f32) + e_rz[0].astype(f32) + e_rz[1].astype(f32)
            + e_rz[2].astype(f32))
    row[...] = jnp.where(h == 0, last, fin[...]).astype(bf16)
    tail = copy(row, r.at[core], ws, wr.at[core], (peer, turn))
    other = 1 - core

    def got_row(slot):
        copy(row, r.at[slot], ws, wr.at[slot], (peer, turn), False).wait_recv()

    if odd:
        r[core] = row[...]
        got_row(other)
    else:
        @pl.when(jnp.logical_not(late))
        def _():
            r[core] = row[...]

        @pl.when(gives)
        def _():
            r[1] = row[...]

        @pl.when(jnp.logical_not(gives))
        def _():
            got_row(other)

        @pl.when(late)
        def _():
            got_row(1)
    loop(CK, lambda ck: got(ck, other))
    if not odd:
        @pl.when(late)
        def _():
            def more(ck):
                got(ck, 1)
                result(ck, 1, (beside, h), False).wait_send()
                chunk(ck, 1, xor(blk, p), False).wait_send()

            loop(CK, more)

        @pl.when(gives)
        def _():
            whole(False).wait_send()

        @pl.when(jnp.logical_not(gives))
        def _():
            loop(CK, lambda ck: chunk(ck, 0, m2_to, False).wait_send())
    else:
        loop(CK, lambda ck: chunk(ck, 0, m2_to, False).wait_send())

    def drain(ck):
        def half_(half):
            ahead(ck, False, half).wait_send()
            direct(ck, False, half).wait_send()
            onward(ck, False, half).wait_send()

        loop(2, half_)
        loop(3, lambda k: along(ck, False, k).wait_send())
        result(ck, 0, (peer, flip), False).wait_send()

    loop(CK, drain)

    def ends(k):
        edge(False, k).wait_send()
        edge_z(False, k).wait_send()

    loop(3, ends)
    tail.wait_send()


def call(p, white, table):
    spec = pl.BlockSpec(memory_space=pltpu.VMEM)
    dma = pltpu.SemaphoreType.DMA
    return tuple(pl.pallas_call(
        functools.partial(kernel, p),
        out_shape=[jax.ShapeDtypeStruct((2, 16, 4096), bf16), jax.ShapeDtypeStruct((2, 32, 128), bf16)],
        in_specs=[spec] * 2,
        out_specs=[spec] * 2,
        scratch_shapes=[
                pltpu.VMEM((2, 8, 64, 128), bf16),
            pltpu.VMEM((CK, 2, 8, CH, 128), bf16),
            pltpu.VMEM((2, 8, CH, 128), f32),
            pltpu.VMEM((256, 256), bf16),
            pltpu.VMEM((CK, 2, 4, 64, CC // 2), bf16),
            pltpu.VMEM((32, 128), f32),
            pltpu.VMEM((CK, 2, 64, CC // 2), bf16),
            pltpu.VMEM((CK, 2, 2, 64, CC // 2), bf16),
            pltpu.VMEM((CK, 4, 16, CC), bf16),
            pltpu.VMEM((CK, 3, 16, CC), bf16),
            pltpu.VMEM((16, 4096), bf16),
            pltpu.VMEM((32, 128), bf16),
            pltpu.VMEM((32, 128), f32),
            pltpu.VMEM((32, 128), bf16),
            pltpu.VMEM((3, 32, 128), bf16),
            pltpu.VMEM((32, 128), bf16),
            pltpu.VMEM((3, 32, 128), bf16),
            dma, dma((2, CK)), dma, dma((CK,)),
            dma((CK, 4)), dma((CK, 4)), dma((CK, 4)), dma((CK, 3)), dma((CK, 3)),
            dma((6,)), dma((6,)), dma((2, CK)), dma((2, CK)), dma, dma((2,)),
        ],
        compiler_params=pltpu.CompilerParams(
            collective_id=p - 1, has_side_effects=True, vmem_limit_bytes=32 << 20),
        name="fused",
    )(white, table))


def phase_table(first, count):
    bins = first + jnp.arange(count, dtype=jnp.int32)
    lags = jnp.arange(ROWS, dtype=jnp.int32) - L // 2
    steps = jnp.mod(lags[:, None] * bins[None, :], 2 * NB)
    angle = steps.astype(f32) * (math.pi / NB)
    return jnp.concatenate([jnp.cos(angle), -jnp.sin(angle)], axis=1).astype(bf16)


def whiten(spectra):
    values = spectra.astype(f32)
    power = jnp.sum(values * values, axis=(0, 1)) / spectra.shape[1]
    return (values / jnp.sqrt(power + EPS)).astype(bf16)


def on_device(spectra, pairing):
    blk = lax.axis_index("blk")
    white = whiten(spectra)
    table = phase_table(lax.axis_index("freq") * 128, 128)
    other = pairing[0] + pairing[1] - 31
    z, r = lax.switch(other - 1, [functools.partial(call, p) for p in range(1, 31)], white, table)

    def plain(k):
        return z[k].reshape(16, 64, 64).transpose(0, 2, 1).reshape(16, 4096)

    def mirrored(k):
        return jnp.concatenate([r[k].reshape(1, 4096), z[k, :0:-1]], axis=0)

    core = blk % 2
    role = ((blk & other & -other) != 0).astype(jnp.int32)
    plain_b = jnp.where(other % 2 == 1, core == 1, core != role)
    out_a = jnp.where(core == 0, plain(0), mirrored(0))
    out_b = jnp.where(plain_b, plain(1), mirrored(1))
    lead = pairing[0] == 31
    return jnp.stack([jnp.where(lead, out_a, out_b), jnp.where(lead, out_b, out_a)]).astype(f32)


def solution(mesh):
    in_specs = (P(None, None, "blk", "freq"), P())
    out_specs = P(None, "freq", "blk")
    return jax.shard_map(
        on_device, mesh=mesh, in_specs=in_specs, out_specs=out_specs, check_vma=False
    )
```
